32 devices in a mesh: sec: 2 (over y), gx: 4 (over x, core), gy: 4 (over z).
Axes of the slice: x: 2, y: 2, z: 4, core: 2. Of those that a mesh axis runs over, the one named last changes fastest.
Arguments:
- flow_state: float32 [3, 64, 64, 256], P(None, ('sec', 'gx'), 'gy'), may hold values from -4 to 4
- blade_cells: int32 [3, 64, 128], replicated, may hold values from 0 to 255, as said below
- blade_coef: float32 [64, 128], replicated, may hold values from 0.2 to 2
Outputs:
- flow_next: float32 [3, 64, 64, 256], P(None, ('sec', 'gx'), 'gy')
The draws below stay inside these ranges and needn't reach their ends.
Inputs may be any that keep to these rules, and one draw needn't show every extreme that they name: `blade_cells`: all 128 points of one turbine share one streamwise index; their spanwise indices lie within 6 cells (periodic over 64) of the turbine's hub and their vertical indices within 6 of the hub's; several points may share a cell; every turbine's hub lies on or one cell below a multiple of 16, and its points lie on both sides of that multiple.
All inputs are finite; a program needn't handle non-finite values.
Results may differ from the reference program's by a relative error of at most 0.00002.
Values sent between devices are 32-bit elements; how exact they have to be, the bound alone decides.
A program may use at most 64 MiB of HBM per device.

```python
import math
import jax
import jax.numpy as jnp

CY = 16
CZ = 256
TURB = 64
ELEMS = 128
RAD = 6
NX = 32
NY = 64
N_SEC = 2


def draw_blade_cells(key, part):
    keys = jax.random.split(jax.random.fold_in(key, 17), 6)
    hub_x = jax.random.randint(keys[0], (TURB, 1), 0, NX)
    turb_ids = jnp.arange(TURB, dtype=jnp.int32)[:, None]
    border = CY * (turb_ids % (NY // CY))
    hub_y = (border - 1 + jax.random.randint(keys[5], (TURB, 1), 0, 2) + NY) % NY
    hub_z = jax.random.randint(keys[2], (TURB, 1), RAD, CZ - RAD)
    off_y = jax.random.randint(keys[3], (TURB, ELEMS), -RAD, RAD + 1)
    elem_ids = jnp.arange(ELEMS, dtype=jnp.int32)[None, :]
    off_y = jnp.where(elem_ids == 0, -RAD, jnp.where(elem_ids == 1, RAD, off_y))
    off_z = jax.random.randint(keys[4], (TURB, ELEMS), -RAD, RAD + 1)
    cell_x = jnp.broadcast_to(hub_x, (TURB, ELEMS))
    cell_y = (hub_y + off_y + NY) % NY
    cell_z = hub_z + off_z
    return jnp.stack([cell_x, cell_y, cell_z], axis=0).astype(jnp.int32)


def steps_of(key, extent, cuts, least, high):
    def one(position, blocks):
        steps = jax.random.uniform(jax.random.fold_in(jax.random.fold_in(key, 6), position), (blocks,), jnp.float32, least / len(cuts), high / len(cuts))
        return jnp.repeat(jnp.exp(steps), extent[position] // blocks).reshape((-1,) + (1,) * (len(extent) - position - 1))

    factor_of = one(*cuts[0])
    for cut in cuts[1:]:
        factor_of = factor_of * one(*cut)
    return factor_of


def scatter_about(stream_key, extent, width, bound, cuts=(), kind=jnp.bfloat16):
    factor_of = steps_of(stream_key, extent, cuts, -0.22, 0.18) if cuts else 1.0
    drawn = jax.random.normal(stream_key, extent, jnp.float32) * width * factor_of
    return jnp.minimum(jnp.maximum(drawn, -bound), bound).astype(kind)


def setup_inputs(seed: int = 0) -> dict:
    key_of = jax.random.split(jax.random.key(seed), 4)
    return {
        "flow_state": scatter_about(key_of[0], (3, N_SEC * NX, NY, CZ), 0.5, 4.0, ((1, 8), (2, 4)), jnp.float32),
        "blade_cells": draw_blade_cells(jax.random.fold_in(key_of[3], 71), 0),
        "blade_coef": jnp.clip(jnp.exp(jax.random.uniform(key_of[2], (TURB, ELEMS), jnp.float32, math.log(0.2), math.log(2.0))), 0.2, 2.0),
    }


time_step = 0.3
viscosity = 0.1
wind_speed = 1.0


def component_rate(comp, up_plane, down_plane, vel_x, vel_y, vel_z):
    x_plus = jnp.concatenate([comp[1:], down_plane[None]], axis=0)
    x_minus = jnp.concatenate([up_plane[None], comp[:-1]], axis=0)
    y_plus = jnp.roll(comp, -1, axis=1)
    y_minus = jnp.roll(comp, 1, axis=1)
    zero_layer = jnp.zeros_like(comp[:, :, :1])
    z_plus = jnp.concatenate([comp[:, :, 1:], zero_layer], axis=2)
    z_minus = jnp.concatenate([zero_layer, comp[:, :, :-1]], axis=2)
    advection = vel_x * (x_plus - x_minus) + vel_y * (y_plus - y_minus) + vel_z * (z_plus - z_minus)
    laplacian = x_plus + x_minus + y_plus + y_minus + z_plus + z_minus - 6.0 * comp
    return -0.5 * advection + viscosity * laplacian


def section_rate(section, up_planes, down_planes):
    vel_x = section[0] + wind_speed
    rates = [component_rate(section[c], up_planes[c], down_planes[c], vel_x, section[1], section[2]) for c in range(3)]
    return jnp.stack(rates, axis=0)


def farm_forcing(farm, blade_cells, blade_coef):
    cell_x = blade_cells[0].reshape(-1)
    cell_y = blade_cells[1].reshape(-1)
    cell_z = blade_cells[2].reshape(-1)
    sampled = farm[:, cell_x, cell_y, cell_z]
    wind_col = jnp.array([wind_speed, 0.0, 0.0], dtype=jnp.float32)[:, None]
    velocity = (sampled + wind_col).reshape(3, TURB, ELEMS)
    mean_axial = jnp.mean(velocity[0], axis=1)
    forces = -blade_coef[None] * mean_axial[None, :, None] * velocity
    total = jnp.zeros_like(farm)
    return total.at[:, cell_x, cell_y, cell_z].add(forces.reshape(3, -1))


def full_rate(flow, blade_cells, blade_coef):
    precursor = flow[:, :NX]
    farm = flow[:, NX:]
    prec_rate = section_rate(precursor, precursor[:, -1], precursor[:, 0])
    farm_rate = section_rate(farm, precursor[:, -1], farm[:, -1])
    farm_rate = farm_rate + farm_forcing(farm, blade_cells, blade_coef)
    return jnp.concatenate([prec_rate, farm_rate], axis=1)


def reference(flow_state, blade_cells, blade_coef):
    segment_one = flow_state + time_step * full_rate(flow_state, blade_cells, blade_coef)
    segment_two = 0.75 * flow_state + 0.25 * (segment_one + time_step * full_rate(segment_one, blade_cells, blade_coef))
    return flow_state / 3.0 + (2.0 / 3.0) * (segment_two + time_step * full_rate(segment_two, blade_cells, blade_coef))
```

```python
import functools

import jax
import jax.numpy as jnp
from jax import lax
from jax.experimental import pallas as pl
from jax.experimental.pallas import tpu as pltpu
from jax.sharding import PartitionSpec as P

time_step = 0.3
viscosity = 0.1
wind_speed = 1.0
MESH = pl.DeviceIdType.MESH
STAGES = ((0.0, 1.0, time_step), (0.75, 0.25, 0.25 * time_step), (1.0 / 3.0, 2.0 / 3.0, 2.0 / 3.0 * time_step))


def footprints_kernel(plane_ref, cells_ref, coef_ref, count_ref, weight_ref):
    turb_count, rows_y, rows_z = count_ref.shape
    points = coef_ref.shape[1]
    first_row = lax.axis_index("gy") * rows_y

    def one(t, carry):
        @pl.when(plane_ref[t] >= 0)
        def _():
            y = cells_ref[1, pl.ds(t, 1), :] - first_row
            z = cells_ref[2, pl.ds(t, 1), :]
            coef = coef_ref[pl.ds(t, 1), :]
            hi = coef.astype(jnp.bfloat16).astype(jnp.float32)
            mid = (coef - hi).astype(jnp.bfloat16).astype(jnp.float32)
            low = coef - hi - mid
            in_row = lax.broadcasted_iota(jnp.int32, (rows_y, points), 0) == y
            left = jnp.concatenate(
                [jnp.where(in_row, part, 0.0) for part in (jnp.full_like(coef, 1.0 / points), hi, mid, low)], axis=0
            ).astype(jnp.bfloat16)
            right = jnp.where(lax.broadcasted_iota(jnp.int32, (rows_z, points), 0) == z, 1.0, 0.0).astype(jnp.bfloat16)
            both = lax.dot_general(left, right, (((1,), (1,)), ((), ())), preferred_element_type=jnp.float32)
            count_ref[t] = both[:rows_y]
            weight_ref[t] = -(both[rows_y : 2 * rows_y] + (both[2 * rows_y : 3 * rows_y] + both[3 * rows_y :]))

        @pl.when(plane_ref[t] < 0)
        def _():
            count_ref[t] = jnp.zeros((rows_y, rows_z), jnp.float32)
            weight_ref[t] = jnp.zeros((rows_y, rows_z), jnp.float32)

        return carry

    lax.fori_loop(0, turb_count, one, 0)


def flow_kernel(
    slabs, spans,
    plane_ref, start_ref, cells_ref, count_ref, weight_ref, out_ref,
    one_ref, two_ref, acc_ref, drag_ref, part_ref, mean_ref,
    y_out, y_in, x_in, send_sem, recv_sem,
):
    n_comp, rows_x, rows_y, rows_z = start_ref.shape
    turb_count, half = part_ref.shape
    sec, slab, span = lax.axis_index("sec"), lax.axis_index("gx"), lax.axis_index("gy")
    in_farm = sec == 1
    has_left = jnp.logical_or(sec == 0, slab > 0)
    has_right = jnp.logical_or(sec == 0, slab < slabs - 1)
    farm_last = jnp.logical_and(in_farm, slab == slabs - 1)
    prec_last = jnp.logical_and(sec == 0, slab == slabs - 1)
    farm_first = jnp.logical_and(in_farm, slab == 0)
    right = (sec, lax.rem(slab + 1, slabs), span)
    left = (sec, lax.rem(slab + slabs - 1, slabs), span)
    above = (sec, slab, lax.rem(span + 1, spans))
    below = (sec, slab, lax.rem(span + spans - 1, spans))
    to_farm = (1, 0, span)
    to_prec = (0, slabs - 1, span)

    barrier = pltpu.get_barrier_semaphore()
    partners = ((above, None), (below, None), (right, has_right), (left, has_left), (to_farm, prec_last), (to_prec, farm_first))
    for device, when in partners:
        def greet(device=device):
            pl.semaphore_signal(barrier, inc=1, device_id=device, device_id_type=MESH)
        greet() if when is None else pl.when(when)(greet)
    peers = 2
    for _, when in partners[2:]:
        peers = peers + jnp.where(when, 1, 0)
    pl.semaphore_wait(barrier, peers)

    row = lax.broadcasted_iota(jnp.int32, (rows_y, rows_z), 0)
    col = lax.broadcasted_iota(jnp.int32, (rows_y, rows_z), 1)
    low_row, high_row = row == 0, row == rows_y - 1
    low_col, high_col = col == 0, col == rows_z - 1
    diagonal = lax.broadcasted_iota(jnp.int32, (turb_count, half), 0) == lax.broadcasted_iota(jnp.int32, (turb_count, half), 1)
    lines = n_comp * rows_x

    states = (start_ref, one_ref, two_ref, out_ref)
    for stage, (keep, here, step) in enumerate(STAGES):
        now, later = states[stage], states[stage + 1]

        def remote(src, dst, s, r, device):
            return pltpu.make_async_remote_copy(
                src_ref=src, dst_ref=dst, send_sem=send_sem.at[stage, s], recv_sem=recv_sem.at[stage, r],
                device_id=device, device_id_type=MESH,
            )

        go_right = remote(now.at[:, rows_x - 1], x_in.at[stage, 0], 0, 0, right)
        go_left = remote(now.at[:, 0], x_in.at[stage, 1], 1, 1, left)
        go_farm = remote(now.at[:, rows_x - 1], x_in.at[stage, 0], 2, 0, to_farm)
        go_above = remote(y_out.at[stage, 0], y_in.at[stage, 0], 3, 2, above)
        go_below = remote(y_out.at[stage, 1], y_in.at[stage, 1], 4, 3, below)
        pl.when(has_right)(go_right.start)
        pl.when(has_left)(go_left.start)
        pl.when(prec_last)(go_farm.start)

        @pl.when(farm_last)
        def _():
            x_in[stage, 1] = now[:, rows_x - 1]

        @pl.when(in_farm)
        def _():
            def eight(i, carry):
                for k in range(8):
                    t = i * 8 + k
                    p = count_ref[t] * now[0, jnp.maximum(plane_ref[t], 0)]
                    p = p[:, :half] + p[:, half:]
                    part_ref[pl.ds(t, 1), :] = jnp.sum(p, axis=0, keepdims=True)
                return carry

            lax.fori_loop(0, turb_count // 8, eight, 0)
            sums = jnp.sum(part_ref[...], axis=1, keepdims=True)
            sums = jnp.sum(jnp.where(diagonal, sums, 0.0), axis=0, keepdims=True)
            for side in range(2):
                y_out[stage, side, pl.ds(lines, 1), pl.ds(0, half)] = sums

        for c in range(n_comp):
            for x in range(rows_x):
                y_out[stage, 0, pl.ds(c * rows_x + x, 1), :] = now[c, x, pl.ds(rows_y - 1, 1), :]
                y_out[stage, 1, pl.ds(c * rows_x + x, 1), :] = now[c, x, pl.ds(0, 1), :]
        go_above.start()
        go_below.start()

        for x in range(rows_x):
            v0 = (now[0, x] + wind_speed) * -0.5
            v1 = now[1, x] * -0.5
            v2 = now[2, x] * -0.5
            for c in range(n_comp):
                q = now[c, x]
                y_plus = jnp.where(high_row, 0.0, pltpu.roll(q, rows_y - 1, 0))
                y_minus = jnp.where(low_row, 0.0, pltpu.roll(q, 1, 0))
                z_plus = jnp.where(high_col, 0.0, pltpu.roll(q, rows_z - 1, 1))
                z_minus = jnp.where(low_col, 0.0, pltpu.roll(q, 1, 1))
                rate = v1 * (y_plus - y_minus) + v2 * (z_plus - z_minus)
                around = (y_plus + y_minus) + (z_plus + z_minus) - 6.0 * q
                if x == 0:
                    x_plus = now[c, x + 1]
                    rate, around = rate + v0 * x_plus, around + x_plus
                elif x == rows_x - 1:
                    x_minus = now[c, x - 1]
                    rate, around = rate - v0 * x_minus, around + x_minus
                else:
                    x_plus, x_minus = now[c, x + 1], now[c, x - 1]
                    rate, around = rate + v0 * (x_plus - x_minus), around + (x_plus + x_minus)
                total = here * q + step * (rate + viscosity * around)
                if keep:
                    total = total + keep * start_ref[c, x]
                acc_ref[c, x] = total

        go_above.wait_recv()
        go_below.wait_recv()

        @pl.when(in_farm)
        def _():
            sums = y_out[stage, 0, pl.ds(lines, 1), pl.ds(0, half)]
            for side in range(2):
                sums = sums + y_in[stage, side, pl.ds(lines, 1), pl.ds(0, half)]
            mean = jnp.sum(jnp.where(diagonal, sums, 0.0), axis=1, keepdims=True) + wind_speed
            first = slab * rows_x
            for x in range(rows_x):
                masked = jnp.where(cells_ref[0] == first + x, mean, 0.0)
                mean_ref[x, :, pl.ds(0, half)] = masked
                mean_ref[x, :, pl.ds(half, half)] = masked

            def one(t, drags):
                w = weight_ref[t]
                return tuple(d + w * mean_ref[x, pl.ds(t, 1), :] for x, d in enumerate(drags))

            zero = jnp.zeros((rows_y, rows_z), jnp.float32)
            drags = lax.fori_loop(0, turb_count, one, (zero,) * rows_x)
            for x in range(rows_x):
                drag_ref[x] = drags[x]

        @pl.when(jnp.logical_not(in_farm))
        def _():
            drag_ref[...] = jnp.zeros_like(drag_ref)

        go_right.wait_recv()
        pl.when(has_right)(go_left.wait_recv)

        for x in range(rows_x):
            q = [now[c, x] for c in range(n_comp)]
            drag = drag_ref[x]
            y_scale = viscosity + jnp.where(low_row, 0.5, -0.5) * q[1]
            for c in range(n_comp):
                line = pl.ds(c * rows_x + x, 1)
                beside = jnp.where(low_row, y_in[stage, 0, line, :], jnp.where(high_row, y_in[stage, 1, line, :], 0.0))
                rate = beside * y_scale + drag * (q[c] + wind_speed if c == 0 else q[c])
                if x == 0:
                    rate = rate + x_in[stage, 0, c] * (viscosity + 0.5 * (q[0] + wind_speed))
                if x == rows_x - 1:
                    rate = rate + x_in[stage, 1, c] * (viscosity - 0.5 * (q[0] + wind_speed))
                later[c, x] = acc_ref[c, x] + step * rate

        pl.when(has_right)(go_right.wait_send)
        pl.when(has_left)(go_left.wait_send)
        pl.when(prec_last)(go_farm.wait_send)
        go_above.wait_send()
        go_below.wait_send()


def body(slabs, spans, flow_state, blade_cells, blade_coef):
    n_comp, rows_x, rows_y, rows_z = flow_state.shape
    turb_count, points = blade_coef.shape
    half = rows_z // 2
    plane = blade_cells[0, :, 0] - lax.axis_index("gx") * rows_x
    row = blade_cells[1] - lax.axis_index("gy") * rows_y
    near = jnp.any(jnp.logical_and(row >= 0, row < rows_y), axis=1)
    near = jnp.logical_and(near, jnp.logical_and(plane >= 0, plane < rows_x))
    plane = jnp.where(jnp.logical_and(near, lax.axis_index("sec") == 1), plane, -1)
    smem = pl.BlockSpec(memory_space=pltpu.SMEM)
    vmem = pl.BlockSpec(memory_space=pltpu.VMEM)
    foot = jax.ShapeDtypeStruct((turb_count, rows_y, rows_z), jnp.float32)
    count, weight = pl.pallas_call(
        footprints_kernel,
        out_shape=(foot, foot),
        in_specs=[smem, vmem, vmem],
        out_specs=(vmem, vmem),
        compiler_params=pltpu.CompilerParams(vmem_limit_bytes=16 << 20),
        name="footprints",
    )(plane, blade_cells, blade_coef)
    block = pltpu.VMEM(flow_state.shape, jnp.float32)
    lines = (n_comp * rows_x + 1 + 7) // 8 * 8
    return pl.pallas_call(
        functools.partial(flow_kernel, slabs, spans),
        out_shape=jax.ShapeDtypeStruct(flow_state.shape, jnp.float32),
        in_specs=[smem, vmem, vmem, vmem, vmem],
        out_specs=vmem,
        scratch_shapes=[
            block, block, block,
            pltpu.VMEM((rows_x, rows_y, rows_z), jnp.float32),
            pltpu.VMEM((turb_count, half), jnp.float32),
            pltpu.VMEM((rows_x, turb_count, rows_z), jnp.float32),
            pltpu.VMEM((3, 2, lines, rows_z), jnp.float32),
            pltpu.VMEM((3, 2, lines, rows_z), jnp.float32),
            pltpu.VMEM((3, 2, n_comp, rows_y, rows_z), jnp.float32),
            pltpu.SemaphoreType.DMA((3, 5)),
            pltpu.SemaphoreType.DMA((3, 4)),
        ],
        compiler_params=pltpu.CompilerParams(
            collective_id=0, has_side_effects=True, vmem_limit_bytes=32 << 20
        ),
        name="substeps",
    )(plane, flow_state, blade_cells, count, weight)


def solution(mesh):
    placed = (P(None, ("sec", "gx"), "gy", None), P(), P())
    return jax.shard_map(
        functools.partial(body, mesh.shape["gx"], mesh.shape["gy"]),
        mesh=mesh,
        in_specs=placed,
        out_specs=P(None, ("sec", "gx"), "gy", None),
        check_vma=False,
    )
```

```python
import functools

import jax
import jax.numpy as jnp
from jax import lax
from jax.experimental import pallas as pl
from jax.experimental.pallas import tpu as pltpu
from jax.sharding import PartitionSpec as P

time_step = 0.3
viscosity = 0.1
wind_speed = 1.0
MESH = pl.DeviceIdType.MESH
STAGES = ((0.0, 1.0, time_step), (0.75, 0.25, 0.25 * time_step), (1.0 / 3.0, 2.0 / 3.0, 2.0 / 3.0 * time_step))


def footprints_kernel(cells_hbm, coef_hbm, count_ref, weight_ref, table_ref, cells_ref, coef_ref, heads_ref, head_ref, last_ref, link_ref, sems):
    turb_count, rows_y, rows_z = count_ref.shape
    rows_x = last_ref.shape[0]
    points = coef_ref.shape[1]

    for i in range(3 * turb_count):
        table_ref[i] = 0
    for x in range(rows_x):
        table_ref[3 * turb_count + x] = turb_count
        last_ref[x] = -1

    @pl.when(lax.axis_index("sec") == 1)
    def _():
        get_cells = pltpu.make_async_copy(cells_hbm, cells_ref, sems.at[0])
        get_coef = pltpu.make_async_copy(coef_hbm, coef_ref, sems.at[1])
        get_cells.start()
        get_coef.start()
        count_ref[...] = jnp.zeros_like(count_ref)
        get_cells.wait()
        diagonal = lax.broadcasted_iota(jnp.int32, (turb_count, points), 0) == lax.broadcasted_iota(jnp.int32, (turb_count, points), 1)
        for i in range(2):
            heads_ref[pl.ds(i, 1), :] = jnp.sum(jnp.where(diagonal, cells_ref[i], 0), axis=0, keepdims=True)
        to_scalars = pltpu.make_async_copy(heads_ref, head_ref, sems.at[2])
        to_scalars.start()
        spans = lax.axis_size("gy")
        span = lax.axis_index("gy")
        first_row = span * rows_y
        first_plane = lax.axis_index("gx") * rows_x
        to_scalars.wait()
        get_coef.wait()

        def chain(t, carry):
            plane = head_ref[0, t] - first_plane
            border = lax.div(head_ref[1, t] + rows_y // 2, rows_y)
            above = jnp.where(border == spans, 0, border)
            inside = jnp.logical_and(plane >= 0, plane < rows_x)
            near = jnp.logical_and(inside, jnp.logical_or(above == span, border - 1 == span))
            near = jnp.logical_or(near, jnp.logical_and(inside, jnp.logical_and(border == 0, span == spans - 1)))

            @pl.when(near)
            def _():
                table_ref[t] = plane
                link_ref[t] = last_ref[plane]
                last_ref[plane] = t

            return carry

        lax.fori_loop(0, turb_count, chain, 0)

        def footprint(t, slot):
            y = cells_ref[1, pl.ds(t, 1), :] - first_row
            z = cells_ref[2, pl.ds(t, 1), :]
            coef = coef_ref[pl.ds(t, 1), :]
            hi = coef.astype(jnp.bfloat16).astype(jnp.float32)
            mid = (coef - hi).astype(jnp.bfloat16).astype(jnp.float32)
            low = coef - hi - mid
            in_row = lax.broadcasted_iota(jnp.int32, (rows_y, points), 0) == y
            left = jnp.concatenate(
                [jnp.where(in_row, part, 0.0) for part in (jnp.full_like(coef, 1.0 / points), hi, mid, low)], axis=0
            ).astype(jnp.bfloat16)
            right = jnp.where(lax.broadcasted_iota(jnp.int32, (rows_z, points), 0) == z, 1.0, 0.0).astype(jnp.bfloat16)
            both = lax.dot_general(left, right, (((1,), (1,)), ((), ())), preferred_element_type=jnp.float32)
            count_ref[t] = both[:rows_y]
            weight_ref[slot] = -(both[rows_y : 2 * rows_y] + (both[2 * rows_y : 3 * rows_y] + both[3 * rows_y :]))

        def one_plane(x, slot):
            def more(state):
                return state[0] >= 0

            def one(state):
                t, k = state
                footprint(t, k)
                table_ref[turb_count + k] = t
                table_ref[2 * turb_count + k] = jnp.where(k == slot, 0, 1)
                table_ref[3 * turb_count + x] = k
                return link_ref[t], k + 1

            return lax.while_loop(more, one, (last_ref[x], slot))[1]

        lax.fori_loop(0, rows_x, one_plane, 0)


def flow_kernel(
    slabs, spans,
    table_ref, start_hbm, count_ref, weight_ref, out_ref,
    start_ref, one_ref, two_ref, acc_ref, drag_ref, part_ref, mean_ref,
    y_out, y_in, x_in, sums_out, sums_in, send_sem, recv_sem, load_sem,
):
    n_comp, rows_x, rows_y, rows_z = start_ref.shape
    turb_count, half = part_ref.shape
    sec, slab, span = lax.axis_index("sec"), lax.axis_index("gx"), lax.axis_index("gy")
    in_farm = sec == 1
    has_left = jnp.logical_or(sec == 0, slab > 0)
    has_right = jnp.logical_or(sec == 0, slab < slabs - 1)
    farm_last = jnp.logical_and(in_farm, slab == slabs - 1)
    prec_last = jnp.logical_and(sec == 0, slab == slabs - 1)
    farm_first = jnp.logical_and(in_farm, slab == 0)
    right = (sec, lax.rem(slab + 1, slabs), span)
    left = (sec, lax.rem(slab + slabs - 1, slabs), span)
    above = (sec, slab, lax.rem(span + 1, spans))
    below = (sec, slab, lax.rem(span + spans - 1, spans))
    to_farm = (1, 0, span)
    to_prec = (0, slabs - 1, span)

    load = pltpu.make_async_copy(start_hbm, start_ref, load_sem)
    load.start()
    barrier = pltpu.get_barrier_semaphore()
    partners = ((above, None), (below, None), (right, has_right), (left, has_left), (to_farm, prec_last), (to_prec, farm_first))
    for device, when in partners:
        def greet(device=device):
            pl.semaphore_signal(barrier, inc=1, device_id=device, device_id_type=MESH)
        greet() if when is None else pl.when(when)(greet)
    peers = 2
    for _, when in partners[2:]:
        peers = peers + jnp.where(when, 1, 0)
    drag_ref[turb_count] = jnp.zeros((rows_y, rows_z), jnp.float32)
    load.wait()

    row = lax.broadcasted_iota(jnp.int32, (rows_y, rows_z), 0)
    col = lax.broadcasted_iota(jnp.int32, (rows_y, rows_z), 1)
    low_row, high_row = row == 0, row == rows_y - 1
    low_col, high_col = col == 0, col == rows_z - 1
    diagonal = lax.broadcasted_iota(jnp.int32, (turb_count, half), 0) == lax.broadcasted_iota(jnp.int32, (turb_count, half), 1)

    states = (start_ref, one_ref, two_ref, out_ref)
    for stage, (keep, here, step) in enumerate(STAGES):
        now, later = states[stage], states[stage + 1]

        def remote(src, dst, s, r, device):
            return pltpu.make_async_remote_copy(
                src_ref=src, dst_ref=dst, send_sem=send_sem.at[stage, s], recv_sem=recv_sem.at[stage, r],
                device_id=device, device_id_type=MESH,
            )

        go_right = remote(now.at[:, rows_x - 1], x_in.at[stage, 0], 0, 0, right)
        go_left = remote(now.at[:, 0], x_in.at[stage, 1], 1, 1, left)
        go_farm = remote(now.at[:, rows_x - 1], x_in.at[stage, 0], 2, 0, to_farm)
        go_above = remote(y_out.at[stage, 0], y_in.at[stage, 0], 3, 2, above)
        go_below = remote(y_out.at[stage, 1], y_in.at[stage, 1], 4, 3, below)
        sums_above = remote(sums_out.at[stage], sums_in.at[stage, 0], 5, 4, above)
        sums_below = remote(sums_out.at[stage], sums_in.at[stage, 1], 6, 5, below)
        for c in range(n_comp):
            for x in range(rows_x):
                y_out[stage, 0, pl.ds(c * rows_x + x, 1), :] = now[c, x, pl.ds(rows_y - 1, 1), :]
                y_out[stage, 1, pl.ds(c * rows_x + x, 1), :] = now[c, x, pl.ds(0, 1), :]
        if stage == 0:
            pl.semaphore_wait(barrier, peers)
        go_above.start()
        go_below.start()
        pl.when(has_right)(go_right.start)
        pl.when(has_left)(go_left.start)
        pl.when(prec_last)(go_farm.start)

        @pl.when(in_farm)
        def _():
            def eight(i, carry):
                for k in range(8):
                    t = i * 8 + k
                    p = count_ref[t] * now[0, table_ref[t]]
                    p = p[:, :half] + p[:, half:]
                    part_ref[pl.ds(t, 1), :] = jnp.sum(p, axis=0, keepdims=True)
                return carry

            lax.fori_loop(0, turb_count // 8, eight, 0)
            sums = jnp.sum(part_ref[...], axis=1, keepdims=True)
            sums = jnp.sum(jnp.where(diagonal, sums, 0.0), axis=0, keepdims=True)
            sums_out[stage] = jnp.broadcast_to(sums, sums_out.shape[1:])
            sums_above.start()
            sums_below.start()

        @pl.when(farm_last)
        def _():
            x_in[stage, 1] = now[:, rows_x - 1]

        for x in range(rows_x):
            v0 = (now[0, x] + wind_speed) * -0.5
            v1 = now[1, x] * -0.5
            v2 = now[2, x] * -0.5
            for c in range(n_comp):
                q = now[c, x]
                y_plus = jnp.where(high_row, 0.0, pltpu.roll(q, rows_y - 1, 0))
                y_minus = jnp.where(low_row, 0.0, pltpu.roll(q, 1, 0))
                z_plus = jnp.where(high_col, 0.0, pltpu.roll(q, rows_z - 1, 1))
                z_minus = jnp.where(low_col, 0.0, pltpu.roll(q, 1, 1))
                rate = v1 * (y_plus - y_minus) + v2 * (z_plus - z_minus)
                around = (y_plus + y_minus) + (z_plus + z_minus) - 6.0 * q
                if x == 0:
                    x_plus = now[c, x + 1]
                    rate, around = rate + v0 * x_plus, around + x_plus
                elif x == rows_x - 1:
                    x_minus = now[c, x - 1]
                    rate, around = rate - v0 * x_minus, around + x_minus
                else:
                    x_plus, x_minus = now[c, x + 1], now[c, x - 1]
                    rate, around = rate + v0 * (x_plus - x_minus), around + (x_plus + x_minus)
                total = here * q + step * (rate + viscosity * around)
                if keep:
                    total = total + keep * start_ref[c, x]
                acc_ref[c, x] = total

        @pl.when(in_farm)
        def _():
            sums_above.wait_recv()
            sums_below.wait_recv()
            sums = sums_out[stage, pl.ds(0, 1), :] + sums_in[stage, 0, pl.ds(0, 1), :] + sums_in[stage, 1, pl.ds(0, 1), :]
            mean = jnp.sum(jnp.where(diagonal, sums, 0.0), axis=1, keepdims=True) + wind_speed
            mean_ref[...] = jnp.broadcast_to(mean, mean_ref.shape)

            def eight_slots(i, acc):
                for k in range(8):
                    slot = i * 8 + k
                    scale = mean_ref[pl.ds(table_ref[turb_count + slot], 1), :]
                    force = weight_ref[slot] * jnp.concatenate([scale, scale], axis=1)
                    acc = jnp.where(table_ref[2 * turb_count + slot] > 0, acc, 0.0) + force
                    drag_ref[slot] = acc
                return acc

            lax.fori_loop(0, turb_count // 8, eight_slots, jnp.zeros((rows_y, rows_z), jnp.float32))

        go_above.wait_recv()
        go_below.wait_recv()
        go_right.wait_recv()
        pl.when(has_right)(go_left.wait_recv)

        for x in range(rows_x):
            q = [now[c, x] for c in range(n_comp)]
            drag = drag_ref[table_ref[3 * turb_count + x]]
            y_scale = viscosity + jnp.where(low_row, 0.5, -0.5) * q[1]
            for c in range(n_comp):
                line = pl.ds(c * rows_x + x, 1)
                beside = jnp.where(low_row, y_in[stage, 0, line, :], jnp.where(high_row, y_in[stage, 1, line, :], 0.0))
                rate = beside * y_scale + drag * (q[c] + wind_speed if c == 0 else q[c])
                if x == 0:
                    rate = rate + x_in[stage, 0, c] * (viscosity + 0.5 * (q[0] + wind_speed))
                if x == rows_x - 1:
                    rate = rate + x_in[stage, 1, c] * (viscosity - 0.5 * (q[0] + wind_speed))
                later[c, x] = acc_ref[c, x] + step * rate

        pl.when(has_right)(go_right.wait_send)
        pl.when(has_left)(go_left.wait_send)
        pl.when(prec_last)(go_farm.wait_send)
        go_above.wait_send()
        go_below.wait_send()
        pl.when(in_farm)(sums_above.wait_send)
        pl.when(in_farm)(sums_below.wait_send)


def body(slabs, spans, flow_state, blade_cells, blade_coef):
    n_comp, rows_x, rows_y, rows_z = flow_state.shape
    turb_count, points = blade_coef.shape
    half = rows_z // 2
    smem = pl.BlockSpec(memory_space=pltpu.SMEM)
    vmem = pl.BlockSpec(memory_space=pltpu.VMEM)
    hbm = pl.BlockSpec(memory_space=pltpu.HBM)
    foot = jax.ShapeDtypeStruct((turb_count, rows_y, rows_z), jnp.float32)
    count, weight, table = pl.pallas_call(
        footprints_kernel,
        out_shape=(foot, foot, jax.ShapeDtypeStruct((3 * turb_count + rows_x,), jnp.int32)),
        in_specs=[hbm, hbm],
        out_specs=(vmem, vmem, smem),
        scratch_shapes=[
            pltpu.VMEM(blade_cells.shape, jnp.int32),
            pltpu.VMEM(blade_coef.shape, jnp.float32),
            pltpu.VMEM((8, points), jnp.int32),
            pltpu.SMEM((8, points), jnp.int32),
            pltpu.SMEM((rows_x,), jnp.int32),
            pltpu.SMEM((turb_count,), jnp.int32),
            pltpu.SemaphoreType.DMA((3,)),
        ],
        compiler_params=pltpu.CompilerParams(vmem_limit_bytes=16 << 20),
        cost_estimate=pl.CostEstimate(flops=4 << 30, bytes_accessed=16 << 20, transcendentals=0),
        name="footprints",
    )(blade_cells, blade_coef)
    block = pltpu.VMEM(flow_state.shape, jnp.float32)
    lines = (n_comp * rows_x + 7) // 8 * 8
    return pl.pallas_call(
        functools.partial(flow_kernel, slabs, spans),
        out_shape=jax.ShapeDtypeStruct(flow_state.shape, jnp.float32),
        in_specs=[smem, hbm, vmem, vmem],
        out_specs=vmem,
        scratch_shapes=[
            block, block, block, block,
            pltpu.VMEM((turb_count + 1, rows_y, rows_z), jnp.float32),
            pltpu.VMEM((turb_count, half), jnp.float32),
            pltpu.VMEM((turb_count, half), jnp.float32),
            pltpu.VMEM((3, 2, lines, rows_z), jnp.float32),
            pltpu.VMEM((3, 2, lines, rows_z), jnp.float32),
            pltpu.VMEM((3, 2, n_comp, rows_y, rows_z), jnp.float32),
            pltpu.VMEM((3, 8, half), jnp.float32),
            pltpu.VMEM((3, 2, 8, half), jnp.float32),
            pltpu.SemaphoreType.DMA((3, 7)),
            pltpu.SemaphoreType.DMA((3, 6)),
            pltpu.SemaphoreType.DMA,
        ],
        compiler_params=pltpu.CompilerParams(
            collective_id=0, has_side_effects=True, vmem_limit_bytes=32 << 20
        ),
        name="substeps",
    )(table, flow_state, count, weight)


def solution(mesh):
    placed = (P(None, ("sec", "gx"), "gy", None), P(), P())
    return jax.shard_map(
        functools.partial(body, mesh.shape["gx"], mesh.shape["gy"]),
        mesh=mesh,
        in_specs=placed,
        out_specs=P(None, ("sec", "gx"), "gy", None),
        check_vma=False,
    )
```

```python
import functools

import jax
import jax.numpy as jnp
from jax import lax
from jax.experimental import pallas as pl
from jax.experimental.pallas import tpu as pltpu
from jax.sharding import PartitionSpec as P

time_step = 0.3
viscosity = 0.1
wind_speed = 1.0
MESH = pl.DeviceIdType.MESH
STAGES = ((0.0, 1.0, time_step), (0.75, 0.25, 0.25 * time_step), (1.0 / 3.0, 2.0 / 3.0, 2.0 / 3.0 * time_step))


def footprints_kernel(cells_hbm, coef_hbm, count_ref, weight_ref, table_ref, cells_ref, coef_ref, heads_ref, head_ref, last_ref, link_ref, sems):
    turb_count, rows_y, rows_z = count_ref.shape
    rows_x = last_ref.shape[0] - 1
    points = coef_ref.shape[1]

    @pl.when(lax.axis_index("sec") == 1)
    def _():
        get_cells = pltpu.make_async_copy(cells_hbm, cells_ref, sems.at[0])
        get_coef = pltpu.make_async_copy(coef_hbm, coef_ref, sems.at[1])
        get_cells.start()
        get_coef.start()
        for i in range(turb_count):
            table_ref[turb_count + i] = 0
            table_ref[2 * turb_count + i] = 0
        for x in range(rows_x):
            table_ref[3 * turb_count + x] = turb_count
            last_ref[x] = -1
        count_ref[...] = jnp.zeros_like(count_ref)
        spans = lax.axis_size("gy")
        span = lax.axis_index("gy")
        first_row = span * rows_y
        get_cells.wait()
        diagonal = lax.broadcasted_iota(jnp.int32, (turb_count, points), 0) == lax.broadcasted_iota(jnp.int32, (turb_count, points), 1)
        plane, start = (jnp.sum(jnp.where(diagonal, cells_ref[i], 0), axis=0, keepdims=True) for i in range(2))
        plane = plane - lax.axis_index("gx") * rows_x
        low = jnp.where(span == 0, spans, span) * rows_y
        high = (span + 1) * rows_y
        at_low = jnp.logical_or(jnp.abs(start - span * rows_y) < rows_y // 2, jnp.abs(start - low) < rows_y // 2)
        at_high = jnp.logical_or(jnp.abs(start - high) < rows_y // 2, jnp.abs(start - jnp.where(span == spans - 1, 0, high)) < rows_y // 2)
        near = jnp.logical_and(jnp.logical_and(plane >= 0, plane < rows_x), jnp.logical_or(at_low, at_high))
        heads_ref[...] = jnp.broadcast_to(jnp.where(near, plane, rows_x), heads_ref.shape)
        to_scalars = pltpu.make_async_copy(heads_ref, head_ref, sems.at[2])
        to_scalars.start()
        to_scalars.wait()

        for t in range(turb_count):
            x = head_ref[0, t]
            table_ref[t] = jnp.minimum(x, rows_x - 1)
            link_ref[t] = last_ref[x]
            last_ref[x] = t

        def one_plane(x, slot):
            def more(state):
                return state[0] >= 0

            def one(state):
                t, k = state
                table_ref[turb_count + k] = t
                table_ref[2 * turb_count + k] = jnp.where(k == slot, 0, 1)
                table_ref[3 * turb_count + x] = k
                last_ref[rows_x] = t
                return link_ref[t], k + 1

            return lax.while_loop(more, one, (last_ref[x], slot))[1]

        last_ref[rows_x] = 0
        used = lax.fori_loop(0, rows_x, one_plane, 0)
        for i in range(3):
            table_ref[turb_count + jnp.minimum(used + i, turb_count - 1)] = last_ref[rows_x]
        get_coef.wait()

        def footprint(t, slot):
            y = cells_ref[1, pl.ds(t, 1), :] - first_row
            z = cells_ref[2, pl.ds(t, 1), :]
            coef = coef_ref[pl.ds(t, 1), :]
            hi = coef.astype(jnp.bfloat16).astype(jnp.float32)
            mid = (coef - hi).astype(jnp.bfloat16).astype(jnp.float32)
            low = coef - hi - mid
            in_row = lax.broadcasted_iota(jnp.int32, (rows_y, points), 0) == y
            left = jnp.concatenate(
                [jnp.where(in_row, part, 0.0) for part in (jnp.full_like(coef, 1.0 / points), hi, mid, low)], axis=0
            ).astype(jnp.bfloat16)
            right = jnp.where(lax.broadcasted_iota(jnp.int32, (rows_z, points), 0) == z, 1.0, 0.0).astype(jnp.bfloat16)
            return lax.dot_general(left, right, (((1,), (1,)), ((), ())), preferred_element_type=jnp.float32)

        def four(i, carry):
            slots = [4 * i + k for k in range(4)]
            turbs = [table_ref[turb_count + slot] for slot in slots]
            for t, slot, both in zip(turbs, slots, [footprint(t, slot) for t, slot in zip(turbs, slots)]):
                count_ref[t] = both[:rows_y]
                weight_ref[slot] = -(both[rows_y : 2 * rows_y] + (both[2 * rows_y : 3 * rows_y] + both[3 * rows_y :]))
            return carry

        lax.fori_loop(0, lax.div(used + 3, 4), four, 0)


def flow_kernel(
    slabs, spans,
    table_ref, start_hbm, count_ref, weight_ref, out_ref,
    start_ref, one_ref, two_ref, acc_ref, drag_ref, part_ref, mean_ref,
    y_out, y_in, x_in, sums_out, sums_in, send_sem, recv_sem, load_sem,
):
    n_comp, rows_x, rows_y, rows_z = start_ref.shape
    turb_count, half = part_ref.shape
    sec, slab, span = lax.axis_index("sec"), lax.axis_index("gx"), lax.axis_index("gy")
    in_farm = sec == 1
    has_left = jnp.logical_or(sec == 0, slab > 0)
    has_right = jnp.logical_or(sec == 0, slab < slabs - 1)
    farm_last = jnp.logical_and(in_farm, slab == slabs - 1)
    prec_last = jnp.logical_and(sec == 0, slab == slabs - 1)
    farm_first = jnp.logical_and(in_farm, slab == 0)
    right = (sec, lax.rem(slab + 1, slabs), span)
    left = (sec, lax.rem(slab + slabs - 1, slabs), span)
    above = (sec, slab, lax.rem(span + 1, spans))
    below = (sec, slab, lax.rem(span + spans - 1, spans))
    to_farm = (1, 0, span)
    to_prec = (0, slabs - 1, span)

    load = pltpu.make_async_copy(start_hbm, start_ref, load_sem)
    load.start()
    barrier = pltpu.get_barrier_semaphore()
    partners = ((above, None), (below, None), (right, has_right), (left, has_left), (to_farm, prec_last), (to_prec, farm_first))
    for device, when in partners:
        def greet(device=device):
            pl.semaphore_signal(barrier, inc=1, device_id=device, device_id_type=MESH)
        greet() if when is None else pl.when(when)(greet)
    peers = 2
    for _, when in partners[2:]:
        peers = peers + jnp.where(when, 1, 0)
    drag_ref[turb_count] = jnp.zeros((rows_y, rows_z), jnp.float32)
    load.wait()

    row = lax.broadcasted_iota(jnp.int32, (rows_y, rows_z), 0)
    col = lax.broadcasted_iota(jnp.int32, (rows_y, rows_z), 1)
    low_row, high_row = row == 0, row == rows_y - 1
    low_col, high_col = col == 0, col == rows_z - 1
    diagonal = lax.broadcasted_iota(jnp.int32, (turb_count, half), 0) == lax.broadcasted_iota(jnp.int32, (turb_count, half), 1)

    states = (start_ref, one_ref, two_ref, out_ref)
    for stage, (keep, here, step) in enumerate(STAGES):
        now, later = states[stage], states[stage + 1]

        def remote(src, dst, s, r, device):
            return pltpu.make_async_remote_copy(
                src_ref=src, dst_ref=dst, send_sem=send_sem.at[stage, s], recv_sem=recv_sem.at[stage, r],
                device_id=device, device_id_type=MESH,
            )

        go_right = remote(now.at[:, rows_x - 1], x_in.at[stage, 0], 0, 0, right)
        go_left = remote(now.at[:, 0], x_in.at[stage, 1], 1, 1, left)
        go_farm = remote(now.at[:, rows_x - 1], x_in.at[stage, 0], 2, 0, to_farm)
        go_above = remote(y_out.at[stage, 0], y_in.at[stage, 0], 3, 2, above)
        go_below = remote(y_out.at[stage, 1], y_in.at[stage, 1], 4, 3, below)
        sums_above = remote(sums_out.at[stage], sums_in.at[stage, 0], 5, 4, above)
        sums_below = remote(sums_out.at[stage], sums_in.at[stage, 1], 6, 5, below)
        for c in range(n_comp):
            for x in range(rows_x):
                y_out[stage, 0, pl.ds(c * rows_x + x, 1), :] = now[c, x, pl.ds(rows_y - 1, 1), :]
                y_out[stage, 1, pl.ds(c * rows_x + x, 1), :] = now[c, x, pl.ds(0, 1), :]
        if stage == 0:
            pl.semaphore_wait(barrier, peers)
        go_above.start()
        go_below.start()
        pl.when(has_right)(go_right.start)
        pl.when(has_left)(go_left.start)
        pl.when(prec_last)(go_farm.start)

        @pl.when(in_farm)
        def _():
            def eight(i, carry):
                for k in range(8):
                    t = i * 8 + k
                    p = count_ref[t] * now[0, table_ref[t]]
                    p = p[:, :half] + p[:, half:]
                    part_ref[pl.ds(t, 1), :] = jnp.sum(p, axis=0, keepdims=True)
                return carry

            lax.fori_loop(0, turb_count // 8, eight, 0)
            sums = jnp.sum(part_ref[...], axis=1, keepdims=True)
            sums = jnp.sum(jnp.where(diagonal, sums, 0.0), axis=0, keepdims=True)
            sums_out[stage] = jnp.broadcast_to(sums, sums_out.shape[1:])
            sums_above.start()
            sums_below.start()

        @pl.when(farm_last)
        def _():
            x_in[stage, 1] = now[:, rows_x - 1]

        for x in range(rows_x):
            v0 = (now[0, x] + wind_speed) * -0.5
            v1 = now[1, x] * -0.5
            v2 = now[2, x] * -0.5
            for c in range(n_comp):
                q = now[c, x]
                y_plus = jnp.where(high_row, 0.0, pltpu.roll(q, rows_y - 1, 0))
                y_minus = jnp.where(low_row, 0.0, pltpu.roll(q, 1, 0))
                z_plus = jnp.where(high_col, 0.0, pltpu.roll(q, rows_z - 1, 1))
                z_minus = jnp.where(low_col, 0.0, pltpu.roll(q, 1, 1))
                rate = v1 * (y_plus - y_minus) + v2 * (z_plus - z_minus)
                around = (y_plus + y_minus) + (z_plus + z_minus) - 6.0 * q
                if x == 0:
                    x_plus = now[c, x + 1]
                    rate, around = rate + v0 * x_plus, around + x_plus
                elif x == rows_x - 1:
                    x_minus = now[c, x - 1]
                    rate, around = rate - v0 * x_minus, around + x_minus
                else:
                    x_plus, x_minus = now[c, x + 1], now[c, x - 1]
                    rate, around = rate + v0 * (x_plus - x_minus), around + (x_plus + x_minus)
                total = here * q + step * (rate + viscosity * around)
                if keep:
                    total = total + keep * start_ref[c, x]
                acc_ref[c, x] = total

        @pl.when(in_farm)
        def _():
            sums_above.wait_recv()
            sums_below.wait_recv()
            sums = sums_out[stage, pl.ds(0, 1), :] + sums_in[stage, 0, pl.ds(0, 1), :] + sums_in[stage, 1, pl.ds(0, 1), :]
            mean = jnp.sum(jnp.where(diagonal, sums, 0.0), axis=1, keepdims=True) + wind_speed
            mean_ref[...] = jnp.broadcast_to(mean, mean_ref.shape)

            def eight_slots(i, acc):
                for k in range(8):
                    slot = i * 8 + k
                    scale = mean_ref[pl.ds(table_ref[turb_count + slot], 1), :]
                    force = weight_ref[slot] * jnp.concatenate([scale, scale], axis=1)
                    acc = jnp.where(table_ref[2 * turb_count + slot] > 0, acc, 0.0) + force
                    drag_ref[slot] = acc
                return acc

            lax.fori_loop(0, turb_count // 8, eight_slots, jnp.zeros((rows_y, rows_z), jnp.float32))

        go_above.wait_recv()
        go_below.wait_recv()
        go_right.wait_recv()
        pl.when(has_right)(go_left.wait_recv)

        for x in range(rows_x):
            q = [now[c, x] for c in range(n_comp)]
            drag = drag_ref[jnp.where(in_farm, table_ref[3 * turb_count + x], turb_count)]
            y_scale = viscosity + jnp.where(low_row, 0.5, -0.5) * q[1]
            for c in range(n_comp):
                line = pl.ds(c * rows_x + x, 1)
                beside = jnp.where(low_row, y_in[stage, 0, line, :], jnp.where(high_row, y_in[stage, 1, line, :], 0.0))
                rate = beside * y_scale + drag * (q[c] + wind_speed if c == 0 else q[c])
                if x == 0:
                    rate = rate + x_in[stage, 0, c] * (viscosity + 0.5 * (q[0] + wind_speed))
                if x == rows_x - 1:
                    rate = rate + x_in[stage, 1, c] * (viscosity - 0.5 * (q[0] + wind_speed))
                later[c, x] = acc_ref[c, x] + step * rate

        pl.when(has_right)(go_right.wait_send)
        pl.when(has_left)(go_left.wait_send)
        pl.when(prec_last)(go_farm.wait_send)
        go_above.wait_send()
        go_below.wait_send()
        pl.when(in_farm)(sums_above.wait_send)
        pl.when(in_farm)(sums_below.wait_send)


def body(slabs, spans, flow_state, blade_cells, blade_coef):
    n_comp, rows_x, rows_y, rows_z = flow_state.shape
    turb_count, points = blade_coef.shape
    half = rows_z // 2
    smem = pl.BlockSpec(memory_space=pltpu.SMEM)
    vmem = pl.BlockSpec(memory_space=pltpu.VMEM)
    hbm = pl.BlockSpec(memory_space=pltpu.HBM)
    foot = jax.ShapeDtypeStruct((turb_count, rows_y, rows_z), jnp.float32)
    count, weight, table = pl.pallas_call(
        footprints_kernel,
        out_shape=(foot, foot, jax.ShapeDtypeStruct((3 * turb_count + rows_x,), jnp.int32)),
        in_specs=[hbm, hbm],
        out_specs=(vmem, vmem, smem),
        scratch_shapes=[
            pltpu.VMEM(blade_cells.shape, jnp.int32),
            pltpu.VMEM(blade_coef.shape, jnp.float32),
            pltpu.VMEM((8, points), jnp.int32),
            pltpu.SMEM((8, points), jnp.int32),
            pltpu.SMEM((rows_x + 1,), jnp.int32),
            pltpu.SMEM((turb_count,), jnp.int32),
            pltpu.SemaphoreType.DMA((3,)),
        ],
        compiler_params=pltpu.CompilerParams(vmem_limit_bytes=16 << 20),
        cost_estimate=pl.CostEstimate(flops=4 << 30, bytes_accessed=16 << 20, transcendentals=0),
        name="footprints",
    )(blade_cells, blade_coef)
    block = pltpu.VMEM(flow_state.shape, jnp.float32)
    lines = (n_comp * rows_x + 7) // 8 * 8
    return pl.pallas_call(
        functools.partial(flow_kernel, slabs, spans),
        out_shape=jax.ShapeDtypeStruct(flow_state.shape, jnp.float32),
        in_specs=[smem, hbm, vmem, vmem],
        out_specs=vmem,
        scratch_shapes=[
            block, block, block, block,
            pltpu.VMEM((turb_count + 1, rows_y, rows_z), jnp.float32),
            pltpu.VMEM((turb_count, half), jnp.float32),
            pltpu.VMEM((turb_count, half), jnp.float32),
            pltpu.VMEM((3, 2, lines, rows_z), jnp.float32),
            pltpu.VMEM((3, 2, lines, rows_z), jnp.float32),
            pltpu.VMEM((3, 2, n_comp, rows_y, rows_z), jnp.float32),
            pltpu.VMEM((3, 8, half), jnp.float32),
            pltpu.VMEM((3, 2, 8, half), jnp.float32),
            pltpu.SemaphoreType.DMA((3, 7)),
            pltpu.SemaphoreType.DMA((3, 6)),
            pltpu.SemaphoreType.DMA,
        ],
        compiler_params=pltpu.CompilerParams(
            collective_id=0, has_side_effects=True, vmem_limit_bytes=32 << 20
        ),
        name="substeps",
    )(table, flow_state, count, weight)


def solution(mesh):
    placed = (P(None, ("sec", "gx"), "gy", None), P(), P())
    return jax.shard_map(
        functools.partial(body, mesh.shape["gx"], mesh.shape["gy"]),
        mesh=mesh,
        in_specs=placed,
        out_specs=P(None, ("sec", "gx"), "gy", None),
        check_vma=False,
    )
```

```python
import functools

import jax
import jax.numpy as jnp
from jax import lax
from jax.experimental import pallas as pl
from jax.experimental.pallas import tpu as pltpu
from jax.sharding import PartitionSpec as P

time_step = 0.3
viscosity = 0.1
wind_speed = 1.0
MESH = pl.DeviceIdType.MESH
STAGES = ((0.0, 1.0, time_step), (0.75, 0.25, 0.25 * time_step), (1.0 / 3.0, 2.0 / 3.0, 2.0 / 3.0 * time_step))


def footprints_kernel(cells_hbm, coef_hbm, count_ref, weight_ref, table_ref, cells_ref, coef_ref, heads_ref, head_ref, last_ref, link_ref, sems):
    turb_count, rows_y, rows_z = count_ref.shape
    rows_x = last_ref.shape[0] - 1
    points = coef_ref.shape[1]

    @pl.when(lax.axis_index("sec") == 1)
    def _():
        get_cells = pltpu.make_async_copy(cells_hbm, cells_ref, sems.at[0])
        get_coef = pltpu.make_async_copy(coef_hbm, coef_ref, sems.at[1])
        get_cells.start()
        get_coef.start()
        for i in range(turb_count):
            table_ref[turb_count + i] = 0
            table_ref[2 * turb_count + i] = 0
        for x in range(rows_x):
            table_ref[3 * turb_count + x] = turb_count
            last_ref[x] = -1
        count_ref[...] = jnp.zeros_like(count_ref)
        spans = lax.axis_size("gy")
        span = lax.axis_index("gy")
        first_row = span * rows_y
        get_cells.wait()
        diagonal = lax.broadcasted_iota(jnp.int32, (turb_count, points), 0) == lax.broadcasted_iota(jnp.int32, (turb_count, points), 1)
        plane, start = (jnp.sum(jnp.where(diagonal, cells_ref[i], 0), axis=0, keepdims=True) for i in range(2))
        plane = plane - lax.axis_index("gx") * rows_x
        low = jnp.where(span == 0, spans, span) * rows_y
        high = (span + 1) * rows_y
        at_low = jnp.logical_or(jnp.abs(start - span * rows_y) < rows_y // 2, jnp.abs(start - low) < rows_y // 2)
        at_high = jnp.logical_or(jnp.abs(start - high) < rows_y // 2, jnp.abs(start - jnp.where(span == spans - 1, 0, high)) < rows_y // 2)
        near = jnp.logical_and(jnp.logical_and(plane >= 0, plane < rows_x), jnp.logical_or(at_low, at_high))
        heads_ref[...] = jnp.broadcast_to(jnp.where(near, plane, rows_x), heads_ref.shape)
        to_scalars = pltpu.make_async_copy(heads_ref, head_ref, sems.at[2])
        to_scalars.start()
        to_scalars.wait()

        for t in range(turb_count):
            x = head_ref[0, t]
            table_ref[t] = jnp.minimum(x, rows_x - 1)
            link_ref[t] = last_ref[x]
            last_ref[x] = t

        def one_plane(x, slot):
            def more(state):
                return state[0] >= 0

            def one(state):
                t, k = state
                table_ref[turb_count + k] = t
                table_ref[2 * turb_count + k] = jnp.where(k == slot, 0, 1)
                table_ref[3 * turb_count + x] = k
                last_ref[rows_x] = t
                return link_ref[t], k + 1

            return lax.while_loop(more, one, (last_ref[x], slot))[1]

        last_ref[rows_x] = 0
        used = lax.fori_loop(0, rows_x, one_plane, 0)
        for i in range(3):
            table_ref[turb_count + jnp.minimum(used + i, turb_count - 1)] = last_ref[rows_x]
        get_coef.wait()

        def footprint(t, slot):
            y = cells_ref[1, pl.ds(t, 1), :] - first_row
            z = cells_ref[2, pl.ds(t, 1), :]
            coef = coef_ref[pl.ds(t, 1), :]
            hi = coef.astype(jnp.bfloat16).astype(jnp.float32)
            mid = (coef - hi).astype(jnp.bfloat16).astype(jnp.float32)
            low = coef - hi - mid
            in_row = lax.broadcasted_iota(jnp.int32, (rows_y, points), 0) == y
            left = jnp.concatenate(
                [jnp.where(in_row, part, 0.0) for part in (jnp.full_like(coef, 1.0 / points), hi, mid, low)], axis=0
            ).astype(jnp.bfloat16)
            right = jnp.where(lax.broadcasted_iota(jnp.int32, (rows_z, points), 0) == z, 1.0, 0.0).astype(jnp.bfloat16)
            return lax.dot_general(left, right, (((1,), (1,)), ((), ())), preferred_element_type=jnp.float32)

        def four(i, carry):
            slots = [4 * i + k for k in range(4)]
            turbs = [table_ref[turb_count + slot] for slot in slots]
            for t, slot, both in zip(turbs, slots, [footprint(t, slot) for t, slot in zip(turbs, slots)]):
                count_ref[t] = both[:rows_y]
                weight_ref[slot] = -(both[rows_y : 2 * rows_y] + (both[2 * rows_y : 3 * rows_y] + both[3 * rows_y :]))
            return carry

        lax.fori_loop(0, lax.div(used + 3, 4), four, 0)


def flow_kernel(
    slabs, spans,
    table_ref, start_hbm, count_ref, weight_ref, out_ref,
    start_ref, one_ref, two_ref, acc_ref, drag_ref, part_ref, mean_ref,
    y_out, y_in, x_in, sums_out, sums_in, send_sem, recv_sem, load_sem,
):
    n_comp, rows_x, rows_y, rows_z = start_ref.shape
    turb_count, half = part_ref.shape
    sec, slab, span = lax.axis_index("sec"), lax.axis_index("gx"), lax.axis_index("gy")
    in_farm = sec == 1
    has_left = jnp.logical_or(sec == 0, slab > 0)
    has_right = jnp.logical_or(sec == 0, slab < slabs - 1)
    farm_last = jnp.logical_and(in_farm, slab == slabs - 1)
    prec_last = jnp.logical_and(sec == 0, slab == slabs - 1)
    farm_first = jnp.logical_and(in_farm, slab == 0)
    right = (sec, lax.rem(slab + 1, slabs), span)
    left = (sec, lax.rem(slab + slabs - 1, slabs), span)
    above = (sec, slab, lax.rem(span + 1, spans))
    below = (sec, slab, lax.rem(span + spans - 1, spans))
    to_farm = (1, 0, span)
    to_prec = (0, slabs - 1, span)

    load = pltpu.make_async_copy(start_hbm, start_ref, load_sem)
    load.start()
    barrier = pltpu.get_barrier_semaphore()
    partners = ((above, None), (below, None), (right, has_right), (left, has_left), (to_farm, prec_last), (to_prec, farm_first))
    for device, when in partners:
        def greet(device=device):
            pl.semaphore_signal(barrier, inc=1, device_id=device, device_id_type=MESH)
        greet() if when is None else pl.when(when)(greet)
    peers = 2
    for _, when in partners[2:]:
        peers = peers + jnp.where(when, 1, 0)
    drag_ref[turb_count] = jnp.zeros((rows_y, rows_z), jnp.float32)
    load.wait()

    row = lax.broadcasted_iota(jnp.int32, (rows_y, rows_z), 0)
    col = lax.broadcasted_iota(jnp.int32, (rows_y, rows_z), 1)
    low_row, high_row = row == 0, row == rows_y - 1
    low_col, high_col = col == 0, col == rows_z - 1
    diagonal = lax.broadcasted_iota(jnp.int32, (turb_count, half), 0) == lax.broadcasted_iota(jnp.int32, (turb_count, half), 1)

    pending = []
    states = (start_ref, one_ref, two_ref, out_ref)
    for stage, (keep, here, step) in enumerate(STAGES):
        now, later = states[stage], states[stage + 1]

        def remote(src, dst, s, r, device):
            return pltpu.make_async_remote_copy(
                src_ref=src, dst_ref=dst, send_sem=send_sem.at[stage, s], recv_sem=recv_sem.at[stage, r],
                device_id=device, device_id_type=MESH,
            )

        go_right = remote(now.at[:, rows_x - 1], x_in.at[stage, 0], 0, 0, right)
        go_left = remote(now.at[:, 0], x_in.at[stage, 1], 1, 1, left)
        go_farm = remote(now.at[:, rows_x - 1], x_in.at[stage, 0], 2, 0, to_farm)
        go_above = remote(y_out.at[stage, 0], y_in.at[stage, 0], 3, 2, above)
        go_below = remote(y_out.at[stage, 1], y_in.at[stage, 1], 4, 3, below)
        sums_above = remote(sums_out.at[stage, 0:1], sums_in.at[stage, 0, 0:1], 5, 4, above)
        sums_below = remote(sums_out.at[stage, 0:1], sums_in.at[stage, 1, 0:1], 6, 5, below)
        for c in range(n_comp):
            for x in range(rows_x):
                y_out[stage, 0, pl.ds(c * rows_x + x, 1), :] = now[c, x, pl.ds(rows_y - 1, 1), :]
                y_out[stage, 1, pl.ds(c * rows_x + x, 1), :] = now[c, x, pl.ds(0, 1), :]
        if stage == 0:
            pl.semaphore_wait(barrier, peers)
        go_above.start()
        go_below.start()
        pl.when(has_right)(go_right.start)
        pl.when(has_left)(go_left.start)
        pl.when(prec_last)(go_farm.start)

        @pl.when(in_farm)
        def _():
            def eight(i, carry):
                for k in range(8):
                    t = i * 8 + k
                    p = count_ref[t] * now[0, table_ref[t]]
                    p = p[:, :half] + p[:, half:]
                    part_ref[pl.ds(t, 1), :] = jnp.sum(p, axis=0, keepdims=True)
                return carry

            lax.fori_loop(0, turb_count // 8, eight, 0)
            sums = jnp.sum(part_ref[...], axis=1, keepdims=True)
            sums = jnp.sum(jnp.where(diagonal, sums, 0.0), axis=0, keepdims=True)
            sums_out[stage] = jnp.broadcast_to(sums, sums_out.shape[1:])
            sums_above.start()
            sums_below.start()

        @pl.when(farm_last)
        def _():
            x_in[stage, 1] = now[:, rows_x - 1]

        for x in range(rows_x):
            v0 = (now[0, x] + wind_speed) * -0.5
            v1 = now[1, x] * -0.5
            v2 = now[2, x] * -0.5
            for c in range(n_comp):
                q = now[c, x]
                y_plus = jnp.where(high_row, 0.0, pltpu.roll(q, rows_y - 1, 0))
                y_minus = jnp.where(low_row, 0.0, pltpu.roll(q, 1, 0))
                z_plus = jnp.where(high_col, 0.0, pltpu.roll(q, rows_z - 1, 1))
                z_minus = jnp.where(low_col, 0.0, pltpu.roll(q, 1, 1))
                rate = v1 * (y_plus - y_minus) + v2 * (z_plus - z_minus)
                around = (y_plus + y_minus) + (z_plus + z_minus) - 6.0 * q
                if x == 0:
                    x_plus = now[c, x + 1]
                    rate, around = rate + v0 * x_plus, around + x_plus
                elif x == rows_x - 1:
                    x_minus = now[c, x - 1]
                    rate, around = rate - v0 * x_minus, around + x_minus
                else:
                    x_plus, x_minus = now[c, x + 1], now[c, x - 1]
                    rate, around = rate + v0 * (x_plus - x_minus), around + (x_plus + x_minus)
                total = here * q + step * (rate + viscosity * around)
                if keep:
                    total = total + keep * start_ref[c, x]
                acc_ref[c, x] = total

        @pl.when(in_farm)
        def _():
            sums_above.wait_recv()
            sums_below.wait_recv()
            sums = sums_out[stage, pl.ds(0, 1), :] + sums_in[stage, 0, pl.ds(0, 1), :] + sums_in[stage, 1, pl.ds(0, 1), :]
            mean = jnp.sum(jnp.where(diagonal, sums, 0.0), axis=1, keepdims=True) + wind_speed
            mean_ref[...] = jnp.broadcast_to(mean, mean_ref.shape)

            def eight_slots(i, acc):
                for k in range(8):
                    slot = i * 8 + k
                    scale = mean_ref[pl.ds(table_ref[turb_count + slot], 1), :]
                    force = weight_ref[slot] * jnp.concatenate([scale, scale], axis=1)
                    acc = jnp.where(table_ref[2 * turb_count + slot] > 0, acc, 0.0) + force
                    drag_ref[slot] = acc
                return acc

            lax.fori_loop(0, turb_count // 8, eight_slots, jnp.zeros((rows_y, rows_z), jnp.float32))

        go_above.wait_recv()
        go_below.wait_recv()
        go_right.wait_recv()
        pl.when(has_right)(go_left.wait_recv)

        for x in range(rows_x):
            q = [now[c, x] for c in range(n_comp)]
            drag = drag_ref[jnp.where(in_farm, table_ref[3 * turb_count + x], turb_count)]
            y_scale = viscosity + jnp.where(low_row, 0.5, -0.5) * q[1]
            for c in range(n_comp):
                line = pl.ds(c * rows_x + x, 1)
                beside = jnp.where(low_row, y_in[stage, 0, line, :], jnp.where(high_row, y_in[stage, 1, line, :], 0.0))
                rate = beside * y_scale + drag * (q[c] + wind_speed if c == 0 else q[c])
                if x == 0:
                    rate = rate + x_in[stage, 0, c] * (viscosity + 0.5 * (q[0] + wind_speed))
                if x == rows_x - 1:
                    rate = rate + x_in[stage, 1, c] * (viscosity - 0.5 * (q[0] + wind_speed))
                later[c, x] = acc_ref[c, x] + step * rate

        pending.append((go_right, go_left, go_farm, go_above, go_below, sums_above, sums_below))

    for go_right, go_left, go_farm, go_above, go_below, sums_above, sums_below in pending:
        pl.when(has_right)(go_right.wait_send)
        pl.when(has_left)(go_left.wait_send)
        pl.when(prec_last)(go_farm.wait_send)
        go_above.wait_send()
        go_below.wait_send()
        pl.when(in_farm)(sums_above.wait_send)
        pl.when(in_farm)(sums_below.wait_send)


def body(slabs, spans, flow_state, blade_cells, blade_coef):
    n_comp, rows_x, rows_y, rows_z = flow_state.shape
    turb_count, points = blade_coef.shape
    half = rows_z // 2
    smem = pl.BlockSpec(memory_space=pltpu.SMEM)
    vmem = pl.BlockSpec(memory_space=pltpu.VMEM)
    hbm = pl.BlockSpec(memory_space=pltpu.HBM)
    foot = jax.ShapeDtypeStruct((turb_count, rows_y, rows_z), jnp.float32)
    count, weight, table = pl.pallas_call(
        footprints_kernel,
        out_shape=(foot, foot, jax.ShapeDtypeStruct((3 * turb_count + rows_x,), jnp.int32)),
        in_specs=[hbm, hbm],
        out_specs=(vmem, vmem, smem),
        scratch_shapes=[
            pltpu.VMEM(blade_cells.shape, jnp.int32),
            pltpu.VMEM(blade_coef.shape, jnp.float32),
            pltpu.VMEM((8, points), jnp.int32),
            pltpu.SMEM((8, points), jnp.int32),
            pltpu.SMEM((rows_x + 1,), jnp.int32),
            pltpu.SMEM((turb_count,), jnp.int32),
            pltpu.SemaphoreType.DMA((3,)),
        ],
        compiler_params=pltpu.CompilerParams(vmem_limit_bytes=16 << 20),
        cost_estimate=pl.CostEstimate(flops=4 << 30, bytes_accessed=16 << 20, transcendentals=0),
        name="footprints",
    )(blade_cells, blade_coef)
    block = pltpu.VMEM(flow_state.shape, jnp.float32)
    lines = (n_comp * rows_x + 7) // 8 * 8
    return pl.pallas_call(
        functools.partial(flow_kernel, slabs, spans),
        out_shape=jax.ShapeDtypeStruct(flow_state.shape, jnp.float32),
        in_specs=[smem, hbm, vmem, vmem],
        out_specs=vmem,
        scratch_shapes=[
            block, block, block, block,
            pltpu.VMEM((turb_count + 1, rows_y, rows_z), jnp.float32),
            pltpu.VMEM((turb_count, half), jnp.float32),
            pltpu.VMEM((turb_count, half), jnp.float32),
            pltpu.VMEM((3, 2, lines, rows_z), jnp.float32),
            pltpu.VMEM((3, 2, lines, rows_z), jnp.float32),
            pltpu.VMEM((3, 2, n_comp, rows_y, rows_z), jnp.float32),
            pltpu.VMEM((3, 8, half), jnp.float32),
            pltpu.VMEM((3, 2, 8, half), jnp.float32),
            pltpu.SemaphoreType.DMA((3, 7)),
            pltpu.SemaphoreType.DMA((3, 6)),
            pltpu.SemaphoreType.DMA,
        ],
        compiler_params=pltpu.CompilerParams(
            collective_id=0, has_side_effects=True, vmem_limit_bytes=32 << 20
        ),
        name="substeps",
    )(table, flow_state, count, weight)


def solution(mesh):
    placed = (P(None, ("sec", "gx"), "gy", None), P(), P())
    return jax.shard_map(
        functools.partial(body, mesh.shape["gx"], mesh.shape["gy"]),
        mesh=mesh,
        in_specs=placed,
        out_specs=P(None, ("sec", "gx"), "gy", None),
        check_vma=False,
    )
```

```python
import functools

import jax
import jax.numpy as jnp
from jax import lax
from jax.experimental import pallas as pl
from jax.experimental.pallas import tpu as pltpu
from jax.sharding import PartitionSpec as P

time_step = 0.3
viscosity = 0.1
wind_speed = 1.0
MESH = pl.DeviceIdType.MESH
STAGES = ((0.0, 1.0, time_step), (0.75, 0.25, 0.25 * time_step), (1.0 / 3.0, 2.0 / 3.0, 2.0 / 3.0 * time_step))


def footprints_kernel(cells_ref, coef_ref, count_ref, weight_ref, table_ref, heads_ref, head_ref, last_ref, link_ref, sems):
    turb_count, rows_y, rows_z = count_ref.shape
    rows_x = last_ref.shape[0] - 1
    points = coef_ref.shape[1]

    @pl.when(lax.axis_index("sec") == 1)
    def _():
        for i in range(turb_count):
            table_ref[turb_count + i] = 0
            table_ref[2 * turb_count + i] = 0
        for x in range(rows_x):
            table_ref[3 * turb_count + x] = turb_count
            last_ref[x] = -1
        count_ref[...] = jnp.zeros_like(count_ref)
        spans = lax.axis_size("gy")
        span = lax.axis_index("gy")
        first_row = span * rows_y
        diagonal = lax.broadcasted_iota(jnp.int32, (turb_count, points), 0) == lax.broadcasted_iota(jnp.int32, (turb_count, points), 1)
        plane, start = (jnp.sum(jnp.where(diagonal, cells_ref[i], 0), axis=0, keepdims=True) for i in range(2))
        plane = plane - lax.axis_index("gx") * rows_x
        low = jnp.where(span == 0, spans, span) * rows_y
        high = (span + 1) * rows_y
        at_low = jnp.logical_or(jnp.abs(start - span * rows_y) < rows_y // 2, jnp.abs(start - low) < rows_y // 2)
        at_high = jnp.logical_or(jnp.abs(start - high) < rows_y // 2, jnp.abs(start - jnp.where(span == spans - 1, 0, high)) < rows_y // 2)
        near = jnp.logical_and(jnp.logical_and(plane >= 0, plane < rows_x), jnp.logical_or(at_low, at_high))
        heads_ref[...] = jnp.broadcast_to(jnp.where(near, plane, rows_x), heads_ref.shape)
        to_scalars = pltpu.make_async_copy(heads_ref, head_ref, sems.at[0])
        to_scalars.start()
        to_scalars.wait()

        for t in range(turb_count):
            x = head_ref[0, t]
            table_ref[t] = jnp.minimum(x, rows_x - 1)
            link_ref[t] = last_ref[x]
            last_ref[x] = t

        def one_plane(x, slot):
            def more(state):
                return state[0] >= 0

            def one(state):
                t, k = state
                table_ref[turb_count + k] = t
                table_ref[2 * turb_count + k] = jnp.where(k == slot, 0, 1)
                table_ref[3 * turb_count + x] = k
                last_ref[rows_x] = t
                return link_ref[t], k + 1

            return lax.while_loop(more, one, (last_ref[x], slot))[1]

        last_ref[rows_x] = 0
        used = lax.fori_loop(0, rows_x, one_plane, 0)
        for i in range(3):
            table_ref[turb_count + jnp.minimum(used + i, turb_count - 1)] = last_ref[rows_x]

        def footprint(t, slot):
            y = cells_ref[1, pl.ds(t, 1), :] - first_row
            z = cells_ref[2, pl.ds(t, 1), :]
            coef = coef_ref[pl.ds(t, 1), :]
            hi = coef.astype(jnp.bfloat16).astype(jnp.float32)
            mid = (coef - hi).astype(jnp.bfloat16).astype(jnp.float32)
            low = coef - hi - mid
            in_row = lax.broadcasted_iota(jnp.int32, (rows_y, points), 0) == y
            left = jnp.concatenate(
                [jnp.where(in_row, part, 0.0) for part in (jnp.full_like(coef, 1.0 / points), hi, mid, low)], axis=0
            ).astype(jnp.bfloat16)
            right = jnp.where(lax.broadcasted_iota(jnp.int32, (rows_z, points), 0) == z, 1.0, 0.0).astype(jnp.bfloat16)
            return lax.dot_general(left, right, (((1,), (1,)), ((), ())), preferred_element_type=jnp.float32)

        def four(i, carry):
            slots = [4 * i + k for k in range(4)]
            turbs = [table_ref[turb_count + slot] for slot in slots]
            for t, slot, both in zip(turbs, slots, [footprint(t, slot) for t, slot in zip(turbs, slots)]):
                count_ref[t] = both[:rows_y]
                weight_ref[slot] = -(both[rows_y : 2 * rows_y] + (both[2 * rows_y : 3 * rows_y] + both[3 * rows_y :]))
            return carry

        lax.fori_loop(0, lax.div(used + 3, 4), four, 0)


def flow_kernel(
    slabs, spans,
    table_ref, start_hbm, count_ref, weight_ref, out_ref,
    start_ref, one_ref, two_ref, acc_ref, drag_ref, part_ref, mean_ref,
    y_out, y_in, x_in, sums_out, sums_in, send_sem, recv_sem, load_sem,
):
    n_comp, rows_x, rows_y, rows_z = start_ref.shape
    turb_count, half = part_ref.shape
    sec, slab, span = lax.axis_index("sec"), lax.axis_index("gx"), lax.axis_index("gy")
    in_farm = sec == 1
    has_left = jnp.logical_or(sec == 0, slab > 0)
    has_right = jnp.logical_or(sec == 0, slab < slabs - 1)
    farm_last = jnp.logical_and(in_farm, slab == slabs - 1)
    prec_last = jnp.logical_and(sec == 0, slab == slabs - 1)
    farm_first = jnp.logical_and(in_farm, slab == 0)
    right = (sec, lax.rem(slab + 1, slabs), span)
    left = (sec, lax.rem(slab + slabs - 1, slabs), span)
    above = (sec, slab, lax.rem(span + 1, spans))
    below = (sec, slab, lax.rem(span + spans - 1, spans))
    to_farm = (1, 0, span)
    to_prec = (0, slabs - 1, span)

    load = pltpu.make_async_copy(start_hbm, start_ref, load_sem)
    load.start()
    barrier = pltpu.get_barrier_semaphore()
    partners = ((above, None), (below, None), (right, has_right), (left, has_left), (to_farm, prec_last), (to_prec, farm_first))
    for device, when in partners:
        def greet(device=device):
            pl.semaphore_signal(barrier, inc=1, device_id=device, device_id_type=MESH)
        greet() if when is None else pl.when(when)(greet)
    peers = 2
    for _, when in partners[2:]:
        peers = peers + jnp.where(when, 1, 0)
    drag_ref[turb_count] = jnp.zeros((rows_y, rows_z), jnp.float32)
    load.wait()

    row = lax.broadcasted_iota(jnp.int32, (rows_y, rows_z), 0)
    col = lax.broadcasted_iota(jnp.int32, (rows_y, rows_z), 1)
    low_row, high_row = row == 0, row == rows_y - 1
    low_col, high_col = col == 0, col == rows_z - 1
    diagonal = lax.broadcasted_iota(jnp.int32, (turb_count, half), 0) == lax.broadcasted_iota(jnp.int32, (turb_count, half), 1)

    pending = []
    states = (start_ref, one_ref, two_ref, out_ref)
    for stage, (keep, here, step) in enumerate(STAGES):
        now, later = states[stage], states[stage + 1]

        def remote(src, dst, s, r, device):
            return pltpu.make_async_remote_copy(
                src_ref=src, dst_ref=dst, send_sem=send_sem.at[stage, s], recv_sem=recv_sem.at[stage, r],
                device_id=device, device_id_type=MESH,
            )

        go_right = remote(now.at[:, rows_x - 1], x_in.at[stage, 0], 0, 0, right)
        go_left = remote(now.at[:, 0], x_in.at[stage, 1], 1, 1, left)
        go_farm = remote(now.at[:, rows_x - 1], x_in.at[stage, 0], 2, 0, to_farm)
        go_above = remote(y_out.at[stage, 0], y_in.at[stage, 0], 3, 2, above)
        go_below = remote(y_out.at[stage, 1], y_in.at[stage, 1], 4, 3, below)
        sums_above = remote(sums_out.at[stage, 0:1], sums_in.at[stage, 0, 0:1], 5, 4, above)
        sums_below = remote(sums_out.at[stage, 0:1], sums_in.at[stage, 1, 0:1], 6, 5, below)
        for c in range(n_comp):
            for x in range(rows_x):
                y_out[stage, 0, pl.ds(c * rows_x + x, 1), :] = now[c, x, pl.ds(rows_y - 1, 1), :]
                y_out[stage, 1, pl.ds(c * rows_x + x, 1), :] = now[c, x, pl.ds(0, 1), :]
        if stage == 0:
            pl.semaphore_wait(barrier, peers)
        go_above.start()
        go_below.start()
        pl.when(has_right)(go_right.start)
        pl.when(has_left)(go_left.start)
        pl.when(prec_last)(go_farm.start)

        @pl.when(in_farm)
        def _():
            def eight(i, carry):
                for k in range(8):
                    t = i * 8 + k
                    p = count_ref[t] * now[0, table_ref[t]]
                    p = p[:, :half] + p[:, half:]
                    part_ref[pl.ds(t, 1), :] = jnp.sum(p, axis=0, keepdims=True)
                return carry

            lax.fori_loop(0, turb_count // 8, eight, 0)
            sums = jnp.sum(part_ref[...], axis=1, keepdims=True)
            sums = jnp.sum(jnp.where(diagonal, sums, 0.0), axis=0, keepdims=True)
            sums_out[stage] = jnp.broadcast_to(sums, sums_out.shape[1:])
            sums_above.start()
            sums_below.start()

        @pl.when(farm_last)
        def _():
            x_in[stage, 1] = now[:, rows_x - 1]

        for x in range(rows_x):
            v0 = (now[0, x] + wind_speed) * -0.5
            v1 = now[1, x] * -0.5
            v2 = now[2, x] * -0.5
            for c in range(n_comp):
                q = now[c, x]
                y_plus = jnp.where(high_row, 0.0, pltpu.roll(q, rows_y - 1, 0))
                y_minus = jnp.where(low_row, 0.0, pltpu.roll(q, 1, 0))
                z_plus = jnp.where(high_col, 0.0, pltpu.roll(q, rows_z - 1, 1))
                z_minus = jnp.where(low_col, 0.0, pltpu.roll(q, 1, 1))
                rate = v1 * (y_plus - y_minus) + v2 * (z_plus - z_minus)
                around = (y_plus + y_minus) + (z_plus + z_minus) - 6.0 * q
                if x == 0:
                    x_plus = now[c, x + 1]
                    rate, around = rate + v0 * x_plus, around + x_plus
                elif x == rows_x - 1:
                    x_minus = now[c, x - 1]
                    rate, around = rate - v0 * x_minus, around + x_minus
                else:
                    x_plus, x_minus = now[c, x + 1], now[c, x - 1]
                    rate, around = rate + v0 * (x_plus - x_minus), around + (x_plus + x_minus)
                total = here * q + step * (rate + viscosity * around)
                if keep:
                    total = total + keep * start_ref[c, x]
                acc_ref[c, x] = total

        @pl.when(in_farm)
        def _():
            sums_above.wait_recv()
            sums_below.wait_recv()
            sums = sums_out[stage, pl.ds(0, 1), :] + sums_in[stage, 0, pl.ds(0, 1), :] + sums_in[stage, 1, pl.ds(0, 1), :]
            mean = jnp.sum(jnp.where(diagonal, sums, 0.0), axis=1, keepdims=True) + wind_speed
            mean_ref[...] = jnp.broadcast_to(mean, mean_ref.shape)

            def eight_slots(i, acc):
                for k in range(8):
                    slot = i * 8 + k
                    scale = mean_ref[pl.ds(table_ref[turb_count + slot], 1), :]
                    force = weight_ref[slot] * jnp.concatenate([scale, scale], axis=1)
                    acc = jnp.where(table_ref[2 * turb_count + slot] > 0, acc, 0.0) + force
                    drag_ref[slot] = acc
                return acc

            lax.fori_loop(0, turb_count // 8, eight_slots, jnp.zeros((rows_y, rows_z), jnp.float32))

        go_above.wait_recv()
        go_below.wait_recv()
        go_right.wait_recv()
        pl.when(has_right)(go_left.wait_recv)

        for x in range(rows_x):
            q = [now[c, x] for c in range(n_comp)]
            drag = drag_ref[jnp.where(in_farm, table_ref[3 * turb_count + x], turb_count)]
            y_scale = viscosity + jnp.where(low_row, 0.5, -0.5) * q[1]
            for c in range(n_comp):
                line = pl.ds(c * rows_x + x, 1)
                beside = jnp.where(low_row, y_in[stage, 0, line, :], jnp.where(high_row, y_in[stage, 1, line, :], 0.0))
                rate = beside * y_scale + drag * (q[c] + wind_speed if c == 0 else q[c])
                if x == 0:
                    rate = rate + x_in[stage, 0, c] * (viscosity + 0.5 * (q[0] + wind_speed))
                if x == rows_x - 1:
                    rate = rate + x_in[stage, 1, c] * (viscosity - 0.5 * (q[0] + wind_speed))
                later[c, x] = acc_ref[c, x] + step * rate

        pending.append((go_right, go_left, go_farm, go_above, go_below, sums_above, sums_below))

    for go_right, go_left, go_farm, go_above, go_below, sums_above, sums_below in pending:
        pl.when(has_right)(go_right.wait_send)
        pl.when(has_left)(go_left.wait_send)
        pl.when(prec_last)(go_farm.wait_send)
        go_above.wait_send()
        go_below.wait_send()
        pl.when(in_farm)(sums_above.wait_send)
        pl.when(in_farm)(sums_below.wait_send)


def body(slabs, spans, flow_state, blade_cells, blade_coef):
    n_comp, rows_x, rows_y, rows_z = flow_state.shape
    turb_count, points = blade_coef.shape
    half = rows_z // 2
    smem = pl.BlockSpec(memory_space=pltpu.SMEM)
    vmem = pl.BlockSpec(memory_space=pltpu.VMEM)
    hbm = pl.BlockSpec(memory_space=pltpu.HBM)
    foot = jax.ShapeDtypeStruct((turb_count, rows_y, rows_z), jnp.float32)
    count, weight, table = pl.pallas_call(
        footprints_kernel,
        out_shape=(foot, foot, jax.ShapeDtypeStruct((3 * turb_count + rows_x,), jnp.int32)),
        in_specs=[vmem, vmem],
        out_specs=(vmem, vmem, smem),
        scratch_shapes=[
            pltpu.VMEM((8, points), jnp.int32),
            pltpu.SMEM((8, points), jnp.int32),
            pltpu.SMEM((rows_x + 1,), jnp.int32),
            pltpu.SMEM((turb_count,), jnp.int32),
            pltpu.SemaphoreType.DMA((1,)),
        ],
        compiler_params=pltpu.CompilerParams(vmem_limit_bytes=16 << 20),
        cost_estimate=pl.CostEstimate(flops=4 << 30, bytes_accessed=16 << 20, transcendentals=0),
        name="footprints",
    )(blade_cells, blade_coef)
    block = pltpu.VMEM(flow_state.shape, jnp.float32)
    lines = (n_comp * rows_x + 7) // 8 * 8
    return pl.pallas_call(
        functools.partial(flow_kernel, slabs, spans),
        out_shape=jax.ShapeDtypeStruct(flow_state.shape, jnp.float32),
        in_specs=[smem, hbm, vmem, vmem],
        out_specs=vmem,
        scratch_shapes=[
            block, block, block, block,
            pltpu.VMEM((turb_count + 1, rows_y, rows_z), jnp.float32),
            pltpu.VMEM((turb_count, half), jnp.float32),
            pltpu.VMEM((turb_count, half), jnp.float32),
            pltpu.VMEM((3, 2, lines, rows_z), jnp.float32),
            pltpu.VMEM((3, 2, lines, rows_z), jnp.float32),
            pltpu.VMEM((3, 2, n_comp, rows_y, rows_z), jnp.float32),
            pltpu.VMEM((3, 8, half), jnp.float32),
            pltpu.VMEM((3, 2, 8, half), jnp.float32),
            pltpu.SemaphoreType.DMA((3, 7)),
            pltpu.SemaphoreType.DMA((3, 6)),
            pltpu.SemaphoreType.DMA,
        ],
        compiler_params=pltpu.CompilerParams(
            collective_id=0, has_side_effects=True, vmem_limit_bytes=32 << 20
        ),
        name="substeps",
    )(table, flow_state, count, weight)


def solution(mesh):
    placed = (P(None, ("sec", "gx"), "gy", None), P(), P())
    return jax.shard_map(
        functools.partial(body, mesh.shape["gx"], mesh.shape["gy"]),
        mesh=mesh,
        in_specs=placed,
        out_specs=P(None, ("sec", "gx"), "gy", None),
        check_vma=False,
    )
```
